512 devices in a mesh: tm: 32 (over z_lo, x), space: 16 (over y, z_hi, core).
Axes of the slice: x: 4, y: 4, z: 16 (z_hi: 2, z_lo: 8; z = z_hi * 8 + z_lo), core: 2. Of those that a mesh axis runs over, the one named last changes fastest.
Arguments:
- base_states: float32 [32, 2, 128, 128, 128], P('tm', None, 'space'), may hold values from 0 to 1
- direction: float32 [32, 2, 128, 128, 128], P('tm', None, 'space'), may hold values from -6 to 6
Outputs:
- product: float32 [32, 2, 128, 128, 128], P('tm', None, 'space')
The draws below stay inside these ranges and needn't reach their ends.
All inputs are finite; a program needn't handle non-finite values.
Results may differ from the reference program's by a relative error of at most 0.00002.
Values sent between devices are 32-bit elements; how exact they have to be, the bound alone decides.
A program may use at most 64 MiB of HBM per device.

```python
import jax
import jax.numpy as jnp
from jax import lax

NY = 128
NX = 128
NZ = 128
SEGS = 32


def levels(stream_key, shape, cuts, least, top_value):
    gain = 1.0
    for position, parts in cuts:
        draws = jax.random.uniform(jax.random.fold_in(jax.random.fold_in(stream_key, 6), position), (parts,), jnp.float32, least / len(cuts), top_value / len(cuts))
        gain = gain * jnp.repeat(jnp.exp(draws), shape[position] // parts).reshape((-1,) + (1,) * (len(shape) - 1 - position))
    return gain


def normal_values(key, shape, scale, bound, cuts=(), dtype=jnp.bfloat16):
    drawn = jax.random.normal(key, shape, jnp.float32) * scale
    if len(cuts) > 0:
        drawn = levels(key, shape, cuts, -0.22, 0.18) * drawn
    return jnp.clip(drawn, min=-bound, max=bound).astype(dtype)


def setup_inputs(seed: int = 0) -> dict:
    splits = jax.random.split(jax.random.key(seed), 3)
    return {
        "base_states": jnp.clip(1.0 * jax.random.uniform(splits[0], (SEGS, 2, NZ, NY, NX), jnp.float32) ** levels(splits[0], (SEGS, 2, NZ, NY, NX), ((0, 32), (2, 16)), -0.2, 0.2), 0.0, 1.0),
        "direction": normal_values(splits[1], (SEGS, 2, NZ, NY, NX), 1.0, 6.0, ((0, 32), (2, 16)), jnp.float32),
    }


diff_substrate = 0.2
diff_catalyst = 0.1
time_step = 0.8
feed_rate = 0.04
kill_rate = 0.06


def laplacian(field):
    total = -6.0 * field
    for axis_id in (1, 2, 3):
        total = total + jnp.roll(field, 1, axis_id) + jnp.roll(field, -1, axis_id)
    return total


def base_advance(state, spread):
    substrate = state[0]
    catalyst = state[1]
    growth = substrate * catalyst * catalyst
    next_substrate = substrate + time_step * (diff_substrate * spread[0] - growth + feed_rate * (1.0 - substrate))
    next_catalyst = catalyst + time_step * (diff_catalyst * spread[1] + growth - (feed_rate + kill_rate) * catalyst)
    return jnp.stack([next_substrate, next_catalyst])


def tangent_advance(state, tangent, spread):
    square = state[1] * state[1]
    cross = 2.0 * state[0] * state[1]
    next_substrate = tangent[0] + time_step * (diff_substrate * spread[0] - (square + feed_rate) * tangent[0] - cross * tangent[1])
    next_catalyst = tangent[1] + time_step * (diff_catalyst * spread[1] + square * tangent[0] + (cross - feed_rate - kill_rate) * tangent[1])
    return jnp.stack([next_substrate, next_catalyst])


def adjoint_advance(state, adjoint, spread):
    square = state[1] * state[1]
    cross = 2.0 * state[0] * state[1]
    next_substrate = adjoint[0] + time_step * (diff_substrate * spread[0] - (square + feed_rate) * adjoint[0] + square * adjoint[1])
    next_catalyst = adjoint[1] + time_step * (diff_catalyst * spread[1] - cross * adjoint[0] + (cross - feed_rate - kill_rate) * adjoint[1])
    return jnp.stack([next_substrate, next_catalyst])


def segment_forward(pair):
    state, tangent = pair
    later_state = base_advance(state, laplacian(state))
    middle = tangent_advance(state, tangent, laplacian(tangent))
    return tangent_advance(later_state, middle, laplacian(middle))


def segment_adjoint(pair):
    state, adjoint = pair
    later_state = base_advance(state, laplacian(state))
    middle = adjoint_advance(later_state, adjoint, laplacian(adjoint))
    return adjoint_advance(state, middle, laplacian(middle))


def reference(base_states, direction):
    images = lax.map(segment_forward, (base_states, direction))
    residual = images - jnp.roll(direction, -1, 0)
    pulled = lax.map(segment_adjoint, (base_states, residual))
    return pulled - jnp.roll(residual, 1, 0)
```

```python
import functools

import jax
import jax.numpy as jnp
from jax import lax
from jax.experimental import pallas as pl
from jax.experimental.pallas import tpu as pltpu
from jax.sharding import PartitionSpec as P

diff_substrate = 0.2
diff_catalyst = 0.1
time_step = 0.8
feed_rate = 0.04
kill_rate = 0.06

MESH = pl.DeviceIdType.MESH
ROW = 4


def laplacian(center, below, above):
    rows, columns = center.shape
    total = -6.0 * center + above + below
    total = total + pltpu.roll(center, 1, 0) + pltpu.roll(center, rows - 1, 0)
    return total + pltpu.roll(center, 1, 1) + pltpu.roll(center, columns - 1, 1)


def base_advance(a, b, spread_a, spread_b):
    growth = a * b * b
    next_a = a + time_step * (diff_substrate * spread_a - growth + feed_rate * (1.0 - a))
    next_b = b + time_step * (diff_catalyst * spread_b + growth - (feed_rate + kill_rate) * b)
    return next_a, next_b


def tangent_advance(a, b, p, q, spread_p, spread_q):
    square = b * b
    cross = 2.0 * a * b
    next_p = p + time_step * (diff_substrate * spread_p - (square + feed_rate) * p - cross * q)
    next_q = q + time_step * (
        diff_catalyst * spread_q + square * p + (cross - feed_rate - kill_rate) * q
    )
    return next_p, next_q


def adjoint_advance(a, b, m, n, spread_m, spread_n):
    square = b * b
    cross = 2.0 * a * b
    next_m = m + time_step * (diff_substrate * spread_m - (square + feed_rate) * m + square * n)
    next_n = n + time_step * (
        diff_catalyst * spread_n - cross * m + (cross - feed_rate - kill_rate) * n
    )
    return next_m, next_n


def kernel(state_hbm, direction_hbm, out_hbm, st, dr, mid, lat, res, adj, out, fol, pri,
           load_sem, store_sem, send_sem, recv_sem):
    depth = lat.shape[0]
    t, s = lax.axis_index("tm"), lax.axis_index("space")
    segments, slabs = lax.axis_size("tm"), lax.axis_size("space")
    up, down = (t, lax.rem(s + 1, slabs)), (t, lax.rem(s + slabs - 1, slabs))
    nxt, prv = (lax.rem(t + 1, segments), s), (lax.rem(t + segments - 1, segments), s)
    wraps = lax.rem(t, ROW) == 0

    barrier = pltpu.get_barrier_semaphore()
    for partner in (up, down, nxt, prv):
        pl.semaphore_signal(barrier, inc=1, device_id=partner, device_id_type=MESH)

    loads = []
    for c in range(2):
        loads.append(pltpu.make_async_copy(
            state_hbm.at[0, c], st.at[pl.ds(1, depth), c], load_sem.at[c]))
        loads.append(pltpu.make_async_copy(
            direction_hbm.at[0, c], dr.at[pl.ds(2, depth), c], load_sem.at[2 + c]))
    for copy in loads:
        copy.start()

    def remote(k, source, target, device):
        return pltpu.make_async_remote_copy(
            src_ref=source, dst_ref=target, send_sem=send_sem.at[k], recv_sem=recv_sem.at[k],
            device_id=device, device_id_type=MESH)

    first = [
        remote(0, st.at[depth], st.at[0], up),
        remote(1, dr.at[pl.ds(depth, 2)], dr.at[pl.ds(0, 2)], up),
        remote(2, st.at[1], st.at[depth + 1], down),
        remote(3, dr.at[pl.ds(2, 2)], dr.at[pl.ds(depth + 2, 2)], down),
    ]
    edges = [
        remote(4, dr.at[2], fol.at[0], prv),
        remote(5, dr.at[depth + 1], fol.at[depth - 1], prv),
    ]
    inner = remote(6, dr.at[pl.ds(3, depth - 2)], fol.at[pl.ds(1, depth - 2)], prv)
    second = [
        remote(7, res.at[depth], res.at[0], up),
        remote(8, res.at[1], res.at[depth + 1], down),
    ]
    third = [
        remote(9, adj.at[depth], adj.at[0], up),
        remote(10, adj.at[1], adj.at[depth + 1], down),
    ]
    bulk = remote(11, res.at[pl.ds(1, depth)], pri, nxt)

    def spread(ref, i):
        return tuple(laplacian(ref[i, c], ref[i - 1, c], ref[i + 1, c]) for c in range(2))

    def later_plane(i):
        lat[i, 0], lat[i, 1] = base_advance(st[i + 1, 0], st[i + 1, 1], *spread(st, i + 1))

    def middle_plane(i):
        mid[i + 1, 0], mid[i + 1, 1] = tangent_advance(
            st[i + 1, 0], st[i + 1, 1], dr[i + 2, 0], dr[i + 2, 1], *spread(dr, i + 2))

    def image_plane(i):
        res[i + 1, 0], res[i + 1, 1] = tangent_advance(
            lat[i, 0], lat[i, 1], mid[i + 1, 0], mid[i + 1, 1], *spread(mid, i + 1))

    def residual_plane(i):
        res[i + 1] = res[i + 1] - fol[i]

    def adjoint_plane(i):
        adj[i + 1, 0], adj[i + 1, 1] = adjoint_advance(
            lat[i, 0], lat[i, 1], res[i + 1, 0], res[i + 1, 1], *spread(res, i + 1))

    def pulled_plane(i):
        out[0, i], out[1, i] = adjoint_advance(
            st[i + 1, 0], st[i + 1, 1], adj[i + 1, 0], adj[i + 1, 1], *spread(adj, i + 1))

    def over(start, stop, *steps):
        @pl.loop(start, stop)
        def _(i):
            for step in steps:
                step(i)

    for copy in loads:
        copy.wait()
    over(1, depth - 1, later_plane, middle_plane)

    pl.semaphore_wait(barrier, 4)
    for copy in first + edges:
        copy.start()

    @pl.when(jnp.logical_not(wraps))
    def _():
        inner.start()

    over(2, depth - 2, image_plane)
    for copy in first:
        copy.wait_send()

    @pl.when(wraps)
    def _():
        inner.start()

    for copy in first:
        copy.wait_recv()
    for i in (0, depth - 1):
        later_plane(i)
    for i in (-1, 0, depth - 1, depth):
        middle_plane(i)
    for i in (0, depth - 1):
        image_plane(i)
    for copy in edges:
        copy.wait()
    for i in (0, depth - 1):
        residual_plane(i)
    for copy in second:
        copy.start()
    for i in (1, depth - 2):
        image_plane(i)
    inner.wait()
    over(1, depth - 1, residual_plane)
    for copy in second:
        copy.wait_send()
    bulk.start()
    over(1, depth - 1, adjoint_plane)
    over(2, depth - 2, pulled_plane)
    for copy in second:
        copy.wait_recv()
    for i in (0, depth - 1):
        adjoint_plane(i)
    for copy in third:
        copy.start()
    for i in (1, depth - 2):
        pulled_plane(i)
    for copy in third:
        copy.wait()
    for i in (0, depth - 1):
        pulled_plane(i)
    bulk.wait()

    @pl.loop(0, depth)
    def _(i):
        for c in range(2):
            out[c, i] = out[c, i] - pri[i, c]

    store = pltpu.make_async_copy(out, out_hbm.at[0], store_sem)
    store.start()
    store.wait()


def local(base_states, direction):
    _, parts, depth, rows, columns = base_states.shape

    def planes(count):
        return pltpu.VMEM((count, parts, rows, columns), jnp.float32)

    return pl.pallas_call(
        kernel,
        out_shape=jax.ShapeDtypeStruct(base_states.shape, jnp.float32),
        in_specs=[pl.BlockSpec(memory_space=pl.ANY)] * 2,
        out_specs=pl.BlockSpec(memory_space=pl.ANY),
        scratch_shapes=[
            planes(depth + 2),
            planes(depth + 4),
            planes(depth + 2),
            planes(depth),
            planes(depth + 2),
            planes(depth + 2),
            pltpu.VMEM((parts, depth, rows, columns), jnp.float32),
            planes(depth),
            planes(depth),
            pltpu.SemaphoreType.DMA((4,)),
            pltpu.SemaphoreType.DMA,
            pltpu.SemaphoreType.DMA((12,)),
            pltpu.SemaphoreType.DMA((12,)),
        ],
        compiler_params=pltpu.CompilerParams(
            collective_id=0, has_side_effects=True, vmem_limit_bytes=40 * 2**20
        ),
    )(base_states, direction)


def solution(mesh):
    spec = P("tm", None, "space", None, None)
    return jax.shard_map(
        local, mesh=mesh, in_specs=(spec, spec), out_specs=spec, check_vma=False
    )
```

```python
import functools

import jax
import jax.numpy as jnp
from jax import lax
from jax.experimental import pallas as pl
from jax.experimental.pallas import tpu as pltpu
from jax.sharding import PartitionSpec as P

diff_substrate = 0.2
diff_catalyst = 0.1
time_step = 0.8
feed_rate = 0.04
kill_rate = 0.06

MESH = pl.DeviceIdType.MESH
ROW = 4


def laplacian(center, below, above):
    rows, columns = center.shape
    total = -6.0 * center + above + below
    total = total + pltpu.roll(center, 1, 0) + pltpu.roll(center, rows - 1, 0)
    return total + pltpu.roll(center, 1, 1) + pltpu.roll(center, columns - 1, 1)


def base_advance(a, b, spread_a, spread_b):
    growth = a * b * b
    next_a = a + time_step * (diff_substrate * spread_a - growth + feed_rate * (1.0 - a))
    next_b = b + time_step * (diff_catalyst * spread_b + growth - (feed_rate + kill_rate) * b)
    return next_a, next_b


def tangent_advance(a, b, p, q, spread_p, spread_q):
    square = b * b
    cross = 2.0 * a * b
    next_p = p + time_step * (diff_substrate * spread_p - (square + feed_rate) * p - cross * q)
    next_q = q + time_step * (
        diff_catalyst * spread_q + square * p + (cross - feed_rate - kill_rate) * q
    )
    return next_p, next_q


def adjoint_advance(a, b, m, n, spread_m, spread_n):
    square = b * b
    cross = 2.0 * a * b
    next_m = m + time_step * (diff_substrate * spread_m - (square + feed_rate) * m + square * n)
    next_n = n + time_step * (
        diff_catalyst * spread_n - cross * m + (cross - feed_rate - kill_rate) * n
    )
    return next_m, next_n


def kernel(state_hbm, direction_hbm, out_hbm, st, dr, mid, lat, res, adj, out, fol, pri, dr_pass,
           res_pass, load_sem, store_sem, send_sem, recv_sem):
    depth = lat.shape[0]
    t, s = lax.axis_index("tm"), lax.axis_index("space")
    segments, slabs = lax.axis_size("tm"), lax.axis_size("space")
    x = lax.rem(t, ROW)
    first_x, last_x = x == 0, x == ROW - 1
    other_x = jnp.logical_not(jnp.logical_or(first_x, last_x))

    def at(steps):
        return (lax.rem(t + steps + segments, segments), s)

    up, down = (t, lax.rem(s + 1, slabs)), (t, lax.rem(s + slabs - 1, slabs))
    nxt, prv = at(1), at(-1)

    def when(condition, *copies):
        @pl.when(condition)
        def _():
            for copy in copies:
                copy.start()

    barrier = pltpu.get_barrier_semaphore()

    def greet(*partners):
        for partner in partners:
            pl.semaphore_signal(barrier, inc=1, device_id=partner, device_id_type=MESH)

    greet(up, down, nxt, prv)

    @pl.when(first_x)
    def _():
        greet(at(ROW - 1), *(at(r - ROW) for r in range(ROW - 1)))

    @pl.when(last_x)
    def _():
        greet(at(1 - ROW), *(at(r + 1) for r in range(1, ROW)))

    @pl.when(other_x)
    def _():
        greet(at(-x), at(ROW - 1 - x))

    loads = []
    for c in range(2):
        loads.append(pltpu.make_async_copy(
            state_hbm.at[0, c], st.at[pl.ds(1, depth), c], load_sem.at[c]))
        loads.append(pltpu.make_async_copy(
            direction_hbm.at[0, c], dr.at[pl.ds(2, depth), c], load_sem.at[2 + c]))
    for copy in loads:
        copy.start()

    def remote(source, target, device, sent, received):
        return pltpu.make_async_remote_copy(
            src_ref=source, dst_ref=target, send_sem=send_sem.at[sent],
            recv_sem=recv_sem.at[received], device_id=device, device_id_type=MESH)

    first = [
        remote(st.at[depth], st.at[0], up, 0, 0),
        remote(dr.at[pl.ds(depth, 2)], dr.at[pl.ds(0, 2)], up, 1, 1),
        remote(st.at[1], st.at[depth + 1], down, 2, 2),
        remote(dr.at[pl.ds(2, 2)], dr.at[pl.ds(depth + 2, 2)], down, 3, 3),
    ]
    second = [
        remote(res.at[depth], res.at[0], up, 4, 4),
        remote(res.at[1], res.at[depth + 1], down, 5, 5),
    ]
    third = [
        remote(adj.at[depth], adj.at[0], up, 6, 6),
        remote(adj.at[1], adj.at[depth + 1], down, 7, 7),
    ]
    edges = [
        remote(dr.at[2], fol.at[0], prv, 8, 8),
        remote(dr.at[depth + 1], fol.at[depth - 1], prv, 9, 9),
    ]

    def part(r):
        return pl.ds(2 * r - 1, 2)

    inner = [
        remote(dr.at[pl.ds(2 * r + 1, 2)], fol.at[part(r)], prv, 9 + r, 9 + r)
        for r in range(1, ROW)
    ]
    inner_by = [
        remote(dr.at[pl.ds(2 * r + 1, 2)], dr_pass, at(r), 9 + r, 13) for r in range(1, ROW)
    ]
    inner_on = [remote(dr_pass, fol.at[part(r)], at(-1 - r), 13, 9 + r) for r in range(1, ROW)]
    bulk = [
        remote(res.at[pl.ds(2 * r + 1, 2)], pri.at[pl.ds(2 * r, 2)], nxt, 14 + r, 14 + r)
        for r in range(ROW)
    ]
    bulk_by = [
        remote(res.at[pl.ds(2 * r + 1, 2)], res_pass, at(r + 1 - ROW), 14 + r, 18)
        for r in range(ROW - 1)
    ]
    bulk_on = [
        remote(res_pass, pri.at[pl.ds(2 * r, 2)], at(ROW - r), 18, 14 + r)
        for r in range(ROW - 1)
    ]

    def spread(ref, i):
        return tuple(laplacian(ref[i, c], ref[i - 1, c], ref[i + 1, c]) for c in range(2))

    def later_plane(i):
        lat[i, 0], lat[i, 1] = base_advance(st[i + 1, 0], st[i + 1, 1], *spread(st, i + 1))

    def middle_plane(i):
        mid[i + 1, 0], mid[i + 1, 1] = tangent_advance(
            st[i + 1, 0], st[i + 1, 1], dr[i + 2, 0], dr[i + 2, 1], *spread(dr, i + 2))

    def image_plane(i):
        res[i + 1, 0], res[i + 1, 1] = tangent_advance(
            lat[i, 0], lat[i, 1], mid[i + 1, 0], mid[i + 1, 1], *spread(mid, i + 1))

    def residual_plane(i):
        res[i + 1] = res[i + 1] - fol[i]

    def adjoint_plane(i):
        adj[i + 1, 0], adj[i + 1, 1] = adjoint_advance(
            lat[i, 0], lat[i, 1], res[i + 1, 0], res[i + 1, 1], *spread(res, i + 1))

    def pulled_plane(i):
        out[0, i], out[1, i] = adjoint_advance(
            st[i + 1, 0], st[i + 1, 1], adj[i + 1, 0], adj[i + 1, 1], *spread(adj, i + 1))

    def over(start, stop, *steps):
        @pl.loop(start, stop)
        def _(i):
            for step in steps:
                step(i)

    for copy in loads:
        copy.wait()
    over(1, depth - 1, later_plane, middle_plane)

    @pl.when(other_x)
    def _():
        pl.semaphore_wait(barrier, 6)

    @pl.when(jnp.logical_not(other_x))
    def _():
        pl.semaphore_wait(barrier, 8)

    for copy in first:
        copy.start()
    when(jnp.logical_not(first_x), *edges, *inner)
    when(first_x, *inner_by)
    over(2, depth - 2, image_plane)
    for copy in first:
        copy.wait_send()
    when(first_x, *edges)
    for r in range(1, ROW):
        @pl.when(x == r)
        def _(r=r):
            inner_by[r - 1].wait_recv()
            inner_on[r - 1].start()

    for side, end in ((0, 0), (1, depth - 1)):
        for copy in first[2 * side:2 * side + 2]:
            copy.wait_recv()
        later_plane(end)
        middle_plane(end)
        middle_plane(end + 2 * side - 1)
        image_plane(end)
        edges[side].wait()
        residual_plane(end)
        second[1 - side].start()
    for i in (1, depth - 2):
        image_plane(i)
    for copy in inner:
        copy.wait()
    over(1, depth - 1, residual_plane)
    when(jnp.logical_not(last_x), *bulk)
    when(last_x, *bulk_by)
    for copy in second:
        copy.wait_send()
    when(last_x, bulk[ROW - 1])
    over(1, depth - 1, adjoint_plane)
    for r in range(ROW - 1):
        @pl.when(x == r)
        def _(r=r):
            bulk_by[r].wait_recv()
            bulk_on[r].start()
    over(2, depth - 2, pulled_plane)
    for side, end in ((0, 0), (1, depth - 1)):
        second[side].wait_recv()
        adjoint_plane(end)
        third[1 - side].start()
    for i in (1, depth - 2):
        pulled_plane(i)
    for side, end in ((0, 0), (1, depth - 1)):
        third[side].wait_recv()
        pulled_plane(end)
    for copy in bulk:
        copy.wait()

    @pl.loop(0, depth)
    def _(i):
        for c in range(2):
            out[c, i] = out[c, i] - pri[i, c]

    store = pltpu.make_async_copy(out, out_hbm.at[0], store_sem)
    store.start()
    for copy in third:
        copy.wait_send()

    @pl.when(jnp.logical_not(first_x))
    def _():
        inner_on[0].wait_send()

    @pl.when(jnp.logical_not(last_x))
    def _():
        bulk_on[0].wait_send()

    store.wait()


def local(base_states, direction):
    _, parts, depth, rows, columns = base_states.shape

    def planes(count):
        return pltpu.VMEM((count, parts, rows, columns), jnp.float32)

    return pl.pallas_call(
        kernel,
        out_shape=jax.ShapeDtypeStruct(base_states.shape, jnp.float32),
        in_specs=[pl.BlockSpec(memory_space=pl.ANY)] * 2,
        out_specs=pl.BlockSpec(memory_space=pl.ANY),
        scratch_shapes=[
            planes(depth + 2),
            planes(depth + 4),
            planes(depth + 2),
            planes(depth),
            planes(depth + 2),
            planes(depth + 2),
            pltpu.VMEM((parts, depth, rows, columns), jnp.float32),
            planes(depth),
            planes(depth),
            planes(2),
            planes(2),
            pltpu.SemaphoreType.DMA((4,)),
            pltpu.SemaphoreType.DMA,
            pltpu.SemaphoreType.DMA((19,)),
            pltpu.SemaphoreType.DMA((19,)),
        ],
        compiler_params=pltpu.CompilerParams(
            collective_id=0, has_side_effects=True, vmem_limit_bytes=40 * 2**20
        ),
    )(base_states, direction)


def solution(mesh):
    spec = P("tm", None, "space", None, None)
    return jax.shard_map(
        local, mesh=mesh, in_specs=(spec, spec), out_specs=spec, check_vma=False
    )
```

```python
import functools

import jax
import jax.numpy as jnp
from jax import lax
from jax.experimental import pallas as pl
from jax.experimental.pallas import tpu as pltpu
from jax.sharding import PartitionSpec as P

diff_substrate = 0.2
diff_catalyst = 0.1
time_step = 0.8
feed_rate = 0.04
kill_rate = 0.06

MESH = pl.DeviceIdType.MESH
ROW = 4
COPIES = 60
EARLY = 0
LOTS = 8
WINDOW = 4
PACED = 3
FOLLOW = (-1, 1, 1, 1)
PRIOR = (0, 0, 0, 0)
BY_FIRST = False
TILE = 8


def pieces(region, rows):
    start, count = region
    start = start % rows
    ahead = min(count, rows - start)
    spans = [(start, ahead)]
    if count > ahead:
        spans.append((0, count - ahead))
    return spans


def take(plane, region):
    spans = pieces(region, plane.shape[0])
    if len(spans) == 1 and spans[0][1] == plane.shape[0]:
        return plane[...]
    values = [plane[pl.ds(start, count)] for start, count in spans]
    return values[0] if len(values) == 1 else jnp.concatenate(values, axis=0)


def put(plane, region, value):
    done = 0
    for start, count in pieces(region, plane.shape[0]):
        plane[pl.ds(start, count)] = value[done:done + count]
        done += count


def laplacian(center, below, above, region):
    rows, columns = center.shape
    start, count = region
    cells = take(center, region)
    total = -6.0 * cells + take(above, region) + take(below, region)
    if count == rows:
        total = total + pltpu.roll(cells, 1, 0) + pltpu.roll(cells, rows - 1, 0)
    else:
        length = count + 2 * TILE
        wide = take(center, (start - TILE, length))
        inside = slice(TILE, TILE + count)
        total = total + pltpu.roll(wide, 1, 0)[inside] + pltpu.roll(wide, length - 1, 0)[inside]
    return total + pltpu.roll(cells, 1, 1) + pltpu.roll(cells, columns - 1, 1)


def base_advance(a, b, spread_a, spread_b):
    growth = a * b * b
    next_a = a + time_step * (diff_substrate * spread_a - growth + feed_rate * (1.0 - a))
    next_b = b + time_step * (diff_catalyst * spread_b + growth - (feed_rate + kill_rate) * b)
    return next_a, next_b


def tangent_advance(a, b, p, q, spread_p, spread_q):
    square = b * b
    cross = 2.0 * a * b
    next_p = p + time_step * (diff_substrate * spread_p - (square + feed_rate) * p - cross * q)
    next_q = q + time_step * (
        diff_catalyst * spread_q + square * p + (cross - feed_rate - kill_rate) * q
    )
    return next_p, next_q


def adjoint_advance(a, b, m, n, spread_m, spread_n):
    square = b * b
    cross = 2.0 * a * b
    next_m = m + time_step * (diff_substrate * spread_m - (square + feed_rate) * m + square * n)
    next_n = n + time_step * (
        diff_catalyst * spread_n - cross * m + (cross - feed_rate - kill_rate) * n
    )
    return next_m, next_n


def kernel(early, state_hbm, direction_hbm, out, st, dr, mid, lat, res, adj, fol, pri,
           dr_pass, res_pass, load_sem, send_sem, recv_sem):
    depth, rows = lat.shape[0], lat.shape[2]
    t, s = lax.axis_index("tm"), lax.axis_index("space")
    segments, slabs = lax.axis_size("tm"), lax.axis_size("space")
    x = lax.rem(t, ROW)
    first_x, last_x = x == 0, x == ROW - 1
    other_x = jnp.logical_not(jnp.logical_or(first_x, last_x))

    def at(steps):
        return (lax.rem(t + steps + segments, segments), s)

    up, down = (t, lax.rem(s + 1, slabs)), (t, lax.rem(s + slabs - 1, slabs))
    nxt, prv = at(1), at(-1)

    whole = (0, rows)
    group = [
        ((start, early - 2 * start), (early - start, rows - early + 2 * start))
        if early else (None, whole)
        for start in (0, TILE, 2 * TILE)
    ]

    def when(condition, *copies):
        @pl.when(condition)
        def _():
            for copy in copies:
                copy.start()

    barrier = pltpu.get_barrier_semaphore()

    def greet(*partners):
        for partner in partners:
            pl.semaphore_signal(barrier, inc=1, device_id=partner, device_id_type=MESH)

    greet(up, down, nxt, prv)

    @pl.when(first_x)
    def _():
        greet(at(ROW - 1), *(at(r - ROW) for r in range(ROW - 1)))

    @pl.when(last_x)
    def _():
        greet(at(1 - ROW), *(at(r + 1) for r in range(1, ROW)))

    @pl.when(other_x)
    def _():
        greet(at(-x), at(ROW - 1 - x))

    loads = []
    for c in range(2):
        loads.append(pltpu.make_async_copy(
            state_hbm.at[0, c], st.at[pl.ds(1, depth), c], load_sem.at[c]))
        loads.append(pltpu.make_async_copy(
            direction_hbm.at[0, c], dr.at[pl.ds(2, depth), c], load_sem.at[2 + c]))
    for copy in loads:
        copy.start()

    def remote(source, target, device, sent, received):
        return pltpu.make_async_remote_copy(
            src_ref=source, dst_ref=target, send_sem=send_sem.at[sent],
            recv_sem=recv_sem.at[received], device_id=device, device_id_type=MESH)

    used = [0]

    def halo(ref, region, count):
        ghosts = (ref.shape[0] - depth) // 2
        spans = pieces(region, rows) if region else []
        sides = []
        for source, target, device in (
            (depth + ghosts - count, ghosts - count, up), (ghosts, depth + ghosts, down)
        ):
            copies = []
            for start, length in spans:
                k = used[0]
                used[0] += 1
                copies.append(remote(
                    ref.at[pl.ds(source, count), :, pl.ds(start, length)],
                    ref.at[pl.ds(target, count), :, pl.ds(start, length)], device, k, k))
            sides.append(copies)
        return sides

    lots = [[p + q for p, q in zip(halo(st, (i * rows // LOTS, rows // LOTS), 1), halo(dr, (i * rows // LOTS, rows // LOTS), 2))] for i in range(LOTS)]
    paced = t >= PACED * ROW
    free = jnp.logical_not(paced)

    halos = [
        [[[], []], [sum((lot[side] for lot in lots), []) for side in range(2)]],
        [halo(res, region, 1) for region in group[1]],
        [halo(adj, region, 1) for region in group[2]],
    ]

    def send(copies):
        for side in copies:
            for copy in side:
                copy.start()

    def sent(copies):
        for side in copies:
            for copy in side:
                copy.wait_send()

    def arrived(copies):
        for copy in copies:
            copy.wait_recv()

    base = used[0]
    edges = [remote(dr.at[i + 2], fol.at[i], prv, base + k, base + k)
             for k, i in enumerate((0, depth - 1))]
    base = base + 2
    follow, follow_by, follow_on = [], [], []
    for r in range(ROW - 1):
        source, target = dr.at[pl.ds(2 * r + 3, 2)], fol.at[pl.ds(2 * r + 1, 2)]
        follow.append(remote(source, target, prv, base + r, base + r))
        follow_by.append(remote(source, dr_pass, at(r + 1), base + r, base + 3))
        follow_on.append(remote(dr_pass, target, at(-2 - r), base + 3, base + r))
    base = base + 4
    prior, prior_by, prior_on = [], [], []
    for r in range(ROW):
        source, target = res.at[pl.ds(2 * r + 1, 2)], pri.at[pl.ds(2 * r, 2)]
        prior.append(remote(source, target, nxt, base + r, base + r))
        prior_by.append(remote(source, res_pass, at(r + 1 - ROW), base + r, base + 4))
        prior_on.append(remote(res_pass, target, at(ROW - r), base + 4, base + r))

    def relay(r, coming, going):
        @pl.when(x == r)
        def _():
            coming.wait_recv()
            going.start()

    def spread(ref, i, region):
        return tuple(
            laplacian(ref.at[i, c], ref.at[i - 1, c], ref.at[i + 1, c], region) for c in range(2))

    def pair(ref, i, region):
        return tuple(take(ref.at[i, c], region) for c in range(2))

    def keep(ref, i, region, values):
        for c in range(2):
            put(ref.at[i, c], region, values[c])

    def later_plane(i, region=whole):
        keep(lat, i, region, base_advance(*pair(st, i + 1, region), *spread(st, i + 1, region)))

    def middle_plane(i, region=whole):
        keep(mid, i + 1, region, tangent_advance(
            *pair(st, i + 1, region), *pair(dr, i + 2, region), *spread(dr, i + 2, region)))

    def image_plane(i, region=whole):
        keep(res, i + 1, region, tangent_advance(
            *pair(lat, i, region), *pair(mid, i + 1, region), *spread(mid, i + 1, region)))

    def residual_plane(i, region=whole):
        keep(res, i + 1, region, tuple(
            value - other for value, other in zip(pair(res, i + 1, region), pair(fol, i, region))))

    def adjoint_plane(i, region=whole):
        keep(adj, i + 1, region, adjoint_advance(
            *pair(lat, i, region), *pair(res, i + 1, region), *spread(res, i + 1, region)))

    def pulled_plane(i):
        values = adjoint_advance(
            *pair(st, i + 1, whole), *pair(adj, i + 1, whole), *spread(adj, i + 1, whole))
        for c in range(2):
            out[0, c, i] = values[c]

    def product_plane(i):
        for c in range(2):
            out[0, c, i] = out[0, c, i] - pri[i, c]

    def over(start, stop, *steps):
        @pl.loop(start, stop)
        def _(i):
            for step in steps:
                step(i)

    sides = ((0, 0, -1), (1, depth - 1, depth))

    def follow_event(now):
        if FOLLOW[0] == now:
            when(first_x, *edges)
        for r in range(ROW - 1):
            if FOLLOW[r + 1] == now:
                relay(r + 1, follow_by[r], follow_on[r])

    def prior_event(now):
        if PRIOR[ROW - 1] == now:
            when(last_x, prior[ROW - 1])
        for r in range(ROW - 1):
            if PRIOR[r] == now:
                relay(r, prior_by[r], prior_on[r])

    for copy in loads:
        copy.wait()
    over(1, depth - 1, later_plane, middle_plane)

    @pl.when(other_x)
    def _():
        pl.semaphore_wait(barrier, 6)

    @pl.when(jnp.logical_not(other_x))
    def _():
        pl.semaphore_wait(barrier, 8)

    follow_event(-1)
    if BY_FIRST:
        when(first_x, *follow_by)
    for lot in lots[:WINDOW]:
        send(lot)
    for lot in lots[WINDOW:]:
        when(free, *lot[0], *lot[1])
    if not BY_FIRST:
        when(first_x, *follow_by)
    when(jnp.logical_not(first_x), *edges, *follow)
    follow_event(0)
    over(2, depth - 2, image_plane)
    follow_event(1)

    @pl.when(paced)
    def _():
        for i in range(WINDOW, LOTS):
            for side in range(2):
                arrived(lots[i - WINDOW][side])
            send(lots[i])


    def first_round(half):
        for side, end, ghost in sides:
            @pl.when(free)
            def _(side=side):
                for lot in lots[:LOTS - WINDOW]:
                    arrived(lot[side])

            for lot in lots[LOTS - WINDOW:]:
                arrived(lot[side])
            later_plane(end, group[0][half])
            middle_plane(end, group[0][half])
            middle_plane(ghost, group[1][half])
            image_plane(end, group[1][half])
            if not half or not early:
                edges[side].wait_recv()
            residual_plane(end, group[1][half])
            for copy in halos[1][half][1 - side]:
                copy.start()

    def second_round(half):
        for side, end, _ in sides:
            arrived(halos[1][half][side])
            adjoint_plane(end, group[2][half])
            for copy in halos[2][half][1 - side]:
                copy.start()

    if early:
        sent(halos[0][0])
        follow_event(2)
        send(halos[0][1])
        follow_event(3)
        first_round(0)
    sent(halos[0][1])
    follow_event(4)
    first_round(1)
    for i in (1, depth - 2):
        image_plane(i)
    for copy in follow:
        copy.wait_recv()
    over(1, depth - 1, residual_plane)
    when(jnp.logical_not(last_x), *prior)
    when(last_x, *prior_by[:ROW - 1])
    prior_event(0)
    if early:
        second_round(0)
    prior_event(1)
    over(1, depth - 1, adjoint_plane)
    sent(halos[1][0])
    sent(halos[1][1])
    prior_event(2)
    over(2, depth - 2, pulled_plane)
    second_round(1)
    for i in (1, depth - 2):
        pulled_plane(i)
    prior_event(3)
    sent(halos[2][0])
    sent(halos[2][1])
    prior_event(4)
    for side, end, _ in sides:
        arrived(halos[2][0][side])
        arrived(halos[2][1][side])
        pulled_plane(end)
    for copy in prior:
        copy.wait_recv()
    over(0, depth, product_plane)
    for copy in edges + follow + prior:
        copy.wait_send()

    @pl.when(jnp.logical_not(first_x))
    def _():
        follow_on[0].wait_send()

    @pl.when(jnp.logical_not(last_x))
    def _():
        prior_on[0].wait_send()


def local(base_states, direction):
    _, parts, depth, rows, columns = base_states.shape

    def planes(count):
        return pltpu.VMEM((count, parts, rows, columns), jnp.float32)

    return pl.pallas_call(
        functools.partial(kernel, rows * EARLY // 16),
        out_shape=jax.ShapeDtypeStruct(base_states.shape, jnp.float32),
        in_specs=[pl.BlockSpec(memory_space=pl.ANY)] * 2,
        out_specs=pl.BlockSpec(memory_space=pltpu.VMEM),
        scratch_shapes=[
            planes(depth + 2),
            planes(depth + 4),
            planes(depth + 2),
            planes(depth),
            planes(depth + 2),
            planes(depth + 2),
            planes(depth),
            planes(depth),
            planes(2),
            planes(2),
            pltpu.SemaphoreType.DMA((4,)),
            pltpu.SemaphoreType.DMA((COPIES,)),
            pltpu.SemaphoreType.DMA((COPIES,)),
        ],
        compiler_params=pltpu.CompilerParams(
            collective_id=0, has_side_effects=True, vmem_limit_bytes=40 * 2**20
        ),
    )(*(pltpu.with_memory_space_constraint(x, pltpu.HBM) for x in (base_states, direction)))


def solution(mesh):
    spec = P("tm", None, "space", None, None)
    return jax.shard_map(
        local, mesh=mesh, in_specs=(spec, spec), out_specs=spec, check_vma=False
    )
```

```python
import functools

import jax
import jax.numpy as jnp
from jax import lax
from jax.experimental import pallas as pl
from jax.experimental.pallas import tpu as pltpu
from jax.sharding import PartitionSpec as P

diff_substrate = 0.2
diff_catalyst = 0.1
time_step = 0.8
feed_rate = 0.04
kill_rate = 0.06

MESH = pl.DeviceIdType.MESH
ROW = 4
COPIES = 60
EARLY = 0
LOTS = 8
WINDOW = 4
PACED = 3
FOLLOW = (-1, 1, 1, 1)
PRIOR = (0, 0, 0, 0)
BY_FIRST = False
TILE = 8


def pieces(region, rows):
    start, count = region
    start = start % rows
    ahead = min(count, rows - start)
    spans = [(start, ahead)]
    if count > ahead:
        spans.append((0, count - ahead))
    return spans


def take(plane, region):
    spans = pieces(region, plane.shape[0])
    if len(spans) == 1 and spans[0][1] == plane.shape[0]:
        return plane[...]
    values = [plane[pl.ds(start, count)] for start, count in spans]
    return values[0] if len(values) == 1 else jnp.concatenate(values, axis=0)


def put(plane, region, value):
    done = 0
    for start, count in pieces(region, plane.shape[0]):
        plane[pl.ds(start, count)] = value[done:done + count]
        done += count


def laplacian(center, below, above, region):
    rows, columns = center.shape
    start, count = region
    cells = take(center, region)
    total = -6.0 * cells + take(above, region) + take(below, region)
    if count == rows:
        total = total + pltpu.roll(cells, 1, 0) + pltpu.roll(cells, rows - 1, 0)
    else:
        length = count + 2 * TILE
        wide = take(center, (start - TILE, length))
        inside = slice(TILE, TILE + count)
        total = total + pltpu.roll(wide, 1, 0)[inside] + pltpu.roll(wide, length - 1, 0)[inside]
    return total + pltpu.roll(cells, 1, 1) + pltpu.roll(cells, columns - 1, 1)


def base_advance(a, b, spread_a, spread_b):
    growth = a * b * b
    next_a = a + time_step * (diff_substrate * spread_a - growth + feed_rate * (1.0 - a))
    next_b = b + time_step * (diff_catalyst * spread_b + growth - (feed_rate + kill_rate) * b)
    return next_a, next_b


def tangent_advance(a, b, p, q, spread_p, spread_q):
    square = b * b
    cross = 2.0 * a * b
    next_p = p + time_step * (diff_substrate * spread_p - (square + feed_rate) * p - cross * q)
    next_q = q + time_step * (
        diff_catalyst * spread_q + square * p + (cross - feed_rate - kill_rate) * q
    )
    return next_p, next_q


def adjoint_advance(a, b, m, n, spread_m, spread_n):
    square = b * b
    cross = 2.0 * a * b
    next_m = m + time_step * (diff_substrate * spread_m - (square + feed_rate) * m + square * n)
    next_n = n + time_step * (
        diff_catalyst * spread_n - cross * m + (cross - feed_rate - kill_rate) * n
    )
    return next_m, next_n


def kernel(early, state_hbm, direction_hbm, out, st, dr, mid, lat, res, adj, fol, pri,
           dr_pass, res_pass, load_sem, send_sem, recv_sem):
    depth, rows = lat.shape[0], lat.shape[2]
    t, s = lax.axis_index("tm"), lax.axis_index("space")
    segments, slabs = lax.axis_size("tm"), lax.axis_size("space")
    x = lax.rem(t, ROW)
    first_x, last_x = x == 0, x == ROW - 1
    other_x = jnp.logical_not(jnp.logical_or(first_x, last_x))

    def at(steps):
        return (lax.rem(t + steps + segments, segments), s)

    up, down = (t, lax.rem(s + 1, slabs)), (t, lax.rem(s + slabs - 1, slabs))
    nxt, prv = at(1), at(-1)

    whole = (0, rows)
    group = [
        ((start, early - 2 * start), (early - start, rows - early + 2 * start))
        if early else (None, whole)
        for start in (0, TILE, 2 * TILE)
    ]

    def when(condition, *copies):
        @pl.when(condition)
        def _():
            for copy in copies:
                copy.start()

    barrier = pltpu.get_barrier_semaphore()

    def greet(*partners):
        for partner in partners:
            pl.semaphore_signal(barrier, inc=1, device_id=partner, device_id_type=MESH)

    greet(up, down, nxt, prv)

    @pl.when(first_x)
    def _():
        greet(at(ROW - 1), *(at(r - ROW) for r in range(ROW - 1)))

    @pl.when(last_x)
    def _():
        greet(at(1 - ROW), *(at(r + 1) for r in range(1, ROW)))

    @pl.when(other_x)
    def _():
        greet(at(-x), at(ROW - 1 - x))

    loads = []
    for c in range(2):
        loads.append(pltpu.make_async_copy(
            state_hbm.at[0, c], st.at[pl.ds(1, depth), c], load_sem.at[c]))
        loads.append(pltpu.make_async_copy(
            direction_hbm.at[0, c], dr.at[pl.ds(2, depth), c], load_sem.at[2 + c]))
    for copy in loads:
        copy.start()

    def remote(source, target, device, sent, received):
        return pltpu.make_async_remote_copy(
            src_ref=source, dst_ref=target, send_sem=send_sem.at[sent],
            recv_sem=recv_sem.at[received], device_id=device, device_id_type=MESH)

    used = [0]

    def halo(ref, region, count):
        ghosts = (ref.shape[0] - depth) // 2
        spans = pieces(region, rows) if region else []
        sides = []
        for source, target, device in (
            (depth + ghosts - count, ghosts - count, up), (ghosts, depth + ghosts, down)
        ):
            copies = []
            for start, length in spans:
                k = used[0]
                used[0] += 1
                copies.append(remote(
                    ref.at[pl.ds(source, count), :, pl.ds(start, length)],
                    ref.at[pl.ds(target, count), :, pl.ds(start, length)], device, k, k))
            sides.append(copies)
        return sides

    lots = [[p + q for p, q in zip(halo(st, (i * rows // LOTS, rows // LOTS), 1), halo(dr, (i * rows // LOTS, rows // LOTS), 2))] for i in range(LOTS)]
    paced = t >= PACED * ROW
    free = jnp.logical_not(paced)

    halos = [
        [[[], []], [sum((lot[side] for lot in lots), []) for side in range(2)]],
        [halo(res, region, 1) for region in group[1]],
        [halo(adj, region, 1) for region in group[2]],
    ]

    def send(copies):
        for side in copies:
            for copy in side:
                copy.start()

    def sent(copies):
        for side in copies:
            for copy in side:
                copy.wait_send()

    def arrived(copies):
        for copy in copies:
            copy.wait_recv()

    base = used[0]
    edges = [remote(dr.at[i + 2], fol.at[i], prv, base + k, base + k)
             for k, i in enumerate((0, depth - 1))]
    base = base + 2
    follow, follow_by, follow_on = [], [], []
    for r in range(ROW - 1):
        source, target = dr.at[pl.ds(2 * r + 3, 2)], fol.at[pl.ds(2 * r + 1, 2)]
        follow.append(remote(source, target, prv, base + r, base + r))
        follow_by.append(remote(source, dr_pass, at(r + 1), base + r, base + 3))
        follow_on.append(remote(dr_pass, target, at(-2 - r), base + 3, base + r))
    base = base + 4
    prior, prior_by, prior_on = [], [], []
    for r in range(ROW):
        source, target = res.at[pl.ds(2 * r + 1, 2)], pri.at[pl.ds(2 * r, 2)]
        prior.append(remote(source, target, nxt, base + r, base + r))
        prior_by.append(remote(source, res_pass, at(r + 1 - ROW), base + r, base + 4))
        prior_on.append(remote(res_pass, target, at(ROW - r), base + 4, base + r))

    def relay(r, coming, going):
        @pl.when(x == r)
        def _():
            coming.wait_recv()
            going.start()

    def spread(ref, i, region):
        return tuple(
            laplacian(ref.at[i, c], ref.at[i - 1, c], ref.at[i + 1, c], region) for c in range(2))

    def pair(ref, i, region):
        return tuple(take(ref.at[i, c], region) for c in range(2))

    def keep(ref, i, region, values):
        for c in range(2):
            put(ref.at[i, c], region, values[c])

    def later_plane(i, region=whole):
        keep(lat, i, region, base_advance(*pair(st, i + 1, region), *spread(st, i + 1, region)))

    def middle_plane(i, region=whole):
        keep(mid, i + 1, region, tangent_advance(
            *pair(st, i + 1, region), *pair(dr, i + 2, region), *spread(dr, i + 2, region)))

    def image_plane(i, region=whole):
        keep(res, i + 1, region, tangent_advance(
            *pair(lat, i, region), *pair(mid, i + 1, region), *spread(mid, i + 1, region)))

    def residual_plane(i, region=whole):
        keep(res, i + 1, region, tuple(
            value - other for value, other in zip(pair(res, i + 1, region), pair(fol, i, region))))

    def adjoint_plane(i, region=whole):
        keep(adj, i + 1, region, adjoint_advance(
            *pair(lat, i, region), *pair(res, i + 1, region), *spread(res, i + 1, region)))

    def pulled_plane(i):
        values = adjoint_advance(
            *pair(st, i + 1, whole), *pair(adj, i + 1, whole), *spread(adj, i + 1, whole))
        for c in range(2):
            out[0, c, i] = values[c]

    def product_plane(i):
        for c in range(2):
            out[0, c, i] = out[0, c, i] - pri[i, c]

    def over(start, stop, *steps):
        @pl.loop(start, stop)
        def _(i):
            for step in steps:
                step(i)

    sides = ((0, 0, -1), (1, depth - 1, depth))

    def follow_event(now):
        if FOLLOW[0] == now:
            when(first_x, *edges)
        for r in range(ROW - 1):
            if FOLLOW[r + 1] == now:
                relay(r + 1, follow_by[r], follow_on[r])

    def prior_event(now):
        if PRIOR[ROW - 1] == now:
            when(last_x, prior[ROW - 1])
        for r in range(ROW - 1):
            if PRIOR[r] == now:
                relay(r, prior_by[r], prior_on[r])

    for copy in loads:
        copy.wait()
    over(1, depth - 1, later_plane, middle_plane)

    @pl.when(other_x)
    def _():
        pl.semaphore_wait(barrier, 6)

    @pl.when(jnp.logical_not(other_x))
    def _():
        pl.semaphore_wait(barrier, 8)

    follow_event(-1)
    if BY_FIRST:
        when(first_x, *follow_by)
    for lot in lots[:WINDOW]:
        send(lot)
    for lot in lots[WINDOW:]:
        when(free, *lot[0], *lot[1])
    if not BY_FIRST:
        when(first_x, *follow_by)
    when(jnp.logical_not(first_x), *edges, *follow)
    follow_event(0)
    over(2, depth - 2, image_plane)
    follow_event(1)

    @pl.when(paced)
    def _():
        for i in range(WINDOW, LOTS):
            for side in range(2):
                arrived(lots[i - WINDOW][side])
            send(lots[i])


    def first_round(half):
        for side, end, ghost in sides:
            @pl.when(free)
            def _(side=side):
                for lot in lots[:LOTS - WINDOW]:
                    arrived(lot[side])

            for lot in lots[LOTS - WINDOW:]:
                arrived(lot[side])
            later_plane(end, group[0][half])
            middle_plane(end, group[0][half])
            middle_plane(ghost, group[1][half])
            image_plane(end, group[1][half])
            if not half or not early:
                edges[side].wait_recv()
            residual_plane(end, group[1][half])
            for copy in halos[1][half][1 - side]:
                copy.start()

    def second_round(half):
        for side, end, _ in sides:
            arrived(halos[1][half][side])
            adjoint_plane(end, group[2][half])
            for copy in halos[2][half][1 - side]:
                copy.start()

    if early:
        sent(halos[0][0])
        follow_event(2)
        send(halos[0][1])
        follow_event(3)
        first_round(0)
    sent(halos[0][1])
    follow_event(4)
    first_round(1)
    for i in (1, depth - 2):
        image_plane(i)
    for copy in follow:
        copy.wait_recv()
    over(1, depth - 1, residual_plane)
    when(jnp.logical_not(last_x), *prior)
    when(last_x, *prior_by[:ROW - 1])
    prior_event(0)
    if early:
        second_round(0)
    prior_event(1)
    over(1, depth - 1, adjoint_plane)
    sent(halos[1][0])
    sent(halos[1][1])
    prior_event(2)
    over(2, depth - 2, pulled_plane)
    second_round(1)
    for i in (1, depth - 2):
        pulled_plane(i)
    prior_event(3)
    sent(halos[2][0])
    sent(halos[2][1])
    prior_event(4)
    for copy in prior:
        copy.wait_recv()
    over(1, depth - 1, product_plane)
    for side, end, _ in sides:
        arrived(halos[2][0][side])
        arrived(halos[2][1][side])
        pulled_plane(end)
        product_plane(end)
    for copy in edges + follow + prior:
        copy.wait_send()

    @pl.when(jnp.logical_not(first_x))
    def _():
        follow_on[0].wait_send()

    @pl.when(jnp.logical_not(last_x))
    def _():
        prior_on[0].wait_send()


def local(base_states, direction):
    _, parts, depth, rows, columns = base_states.shape

    def planes(count):
        return pltpu.VMEM((count, parts, rows, columns), jnp.float32)

    return pl.pallas_call(
        functools.partial(kernel, rows * EARLY // 16),
        out_shape=jax.ShapeDtypeStruct(base_states.shape, jnp.float32),
        in_specs=[pl.BlockSpec(memory_space=pl.ANY)] * 2,
        out_specs=pl.BlockSpec(memory_space=pltpu.VMEM),
        scratch_shapes=[
            planes(depth + 2),
            planes(depth + 4),
            planes(depth + 2),
            planes(depth),
            planes(depth + 2),
            planes(depth + 2),
            planes(depth),
            planes(depth),
            planes(2),
            planes(2),
            pltpu.SemaphoreType.DMA((4,)),
            pltpu.SemaphoreType.DMA((COPIES,)),
            pltpu.SemaphoreType.DMA((COPIES,)),
        ],
        compiler_params=pltpu.CompilerParams(
            collective_id=0, has_side_effects=True, vmem_limit_bytes=40 * 2**20
        ),
    )(*(pltpu.with_memory_space_constraint(x, pltpu.HBM) for x in (base_states, direction)))


def solution(mesh):
    spec = P("tm", None, "space", None, None)
    return jax.shard_map(
        local, mesh=mesh, in_specs=(spec, spec), out_specs=spec, check_vma=False
    )
```
